32 devices in a mesh: groups: 2 (over y), row: 8 (over z, x), col: 2 (over core).
Axes of the slice: x: 2, y: 2, z: 4, core: 2. Of those that a mesh axis runs over, the one named last changes fastest.
Arguments:
- coords: float32 [3, 32768], P(None, ('groups', 'row', 'col')), parts along dimension 1, may hold values from 0 to 24
- atom_types: int32 [32768], P(('groups', 'row', 'col')), parts along dimension 0, may hold values from 0 to 127
- slot_atom: int32 [32768], P(('groups', 'row', 'col')), parts along dimension 0, may hold values from 0 to 1023, as said below
- block_pairs: int32 [2, 4096], P(None, ('groups', 'row', 'col')), parts along dimension 1, may hold values from 0 to 63, as said below
- pair_count: int32 [32], P(('groups', 'row', 'col')), parts along dimension 0, may hold values from 16 to 128, as said below
- exclusion: int32 [256, 64], P(('groups', 'row', 'col')), parts along dimension 0, may hold values from 0 to 1073741823
- sigma_type: float32 [128], replicated, may hold values from 2.5 to 4
- well_type: float32 [128], replicated, may hold values from 0.1 to 0.5
- charge_type: float32 [128], replicated, may hold values from -0.8 to 0.8
Outputs:
- forces: float32 [3, 32768], P(None, ('groups', 'row', 'col')), parts along dimension 1
The draws below stay inside these ranges and needn't reach their ends.
There are 2 independent parts, one for each index of `groups`. The reference program is written for one: setup_inputs(seed, part) draws one part's arguments, and reference() takes and returns one part's arrays. A program takes and returns all parts, laid end to end along the dimension named above; an argument that names none is the same for every part. Nothing has to cross between parts.
Inputs may be any that keep to these rules, and one draw needn't show every extreme that they name: `slot_atom`: the 1024 entries of each device are a permutation of 0 to 1023. `block_pairs`: entry d * 128 + s belongs to device d; row 0 is a block of its row group, below 16; row 1 is a block of its column group whose row index q // 8 differs from the device's own row index. `pair_count`: some device uses all its slots in every draw.
All inputs are finite; a program needn't handle non-finite values.
Results may differ from the reference program's by a relative error of at most 0.0003.
Values sent between devices are 32-bit elements; how exact they have to be, the bound alone decides.
A program may use at most 64 MiB of HBM per device.

```python
import jax
import jax.numpy as jnp
from jax import lax

BLOCK = 128
TYPES = 128
BLK_DEV = 8
ATOM_DEV = 1024
PAIRS_DEV = 128
ROW_BLOCKS = 16
COL_BLOCKS = 64
BLOCKS = 128
ATOMS = 16384
PAIRS = 2048
N_ROW = 8
N_COL = 2


def draw_slot_atom(key, part):
    device_keys = jax.random.split(key, ATOMS // ATOM_DEV)
    shuffled = jax.vmap(lambda device_key: jax.random.permutation(device_key, ATOM_DEV))(device_keys)
    return shuffled.reshape(ATOMS).astype(jnp.int32)


def draw_block_pairs(key, part):
    entry = jnp.arange(PAIRS, dtype=jnp.int32)
    device = entry // PAIRS_DEV
    row_devices = COL_BLOCKS // BLK_DEV
    col_devices = ROW_BLOCKS // BLK_DEV
    row_place = device // col_devices
    first_block = jax.random.randint(jax.random.fold_in(key, 21), (PAIRS,), 0, ROW_BLOCKS)
    row_step = jax.random.randint(jax.random.fold_in(key, 22), (PAIRS,), 1, row_devices)
    other_row = (row_place + row_step) % row_devices
    second_block = other_row * BLK_DEV + jax.random.randint(jax.random.fold_in(key, 23), (PAIRS,), 0, BLK_DEV)
    return jnp.stack([first_block, second_block]).astype(jnp.int32)


def draw_pair_count(key, part):
    devices = PAIRS // PAIRS_DEV
    counts = jax.random.randint(jax.random.fold_in(key, 11), (devices,), PAIRS_DEV // 8, PAIRS_DEV // 2 + 1)
    full_device = jax.random.randint(jax.random.fold_in(key, 12), (), 0, devices)
    return jnp.where(jnp.arange(devices) == full_device, PAIRS_DEV, counts).astype(jnp.int32)


def set_ends(drawn, own_key, low, top_value):
    longest = drawn.shape.index(max(drawn.shape))
    spots = []
    for shift in (0, 1):
        where = [jax.random.randint(jax.random.fold_in(own_key, axis), (), 0, length) for axis, length in enumerate(drawn.shape)]
        where[longest] = (where[longest] + shift) % drawn.shape[longest]
        spots.append(tuple(where))
    return drawn.at[spots[0]].set(low).at[spots[1]].set(top_value)


def block_scale(rng, dims, pieces, smallest, largest):
    loudness = 1.0
    for dim, blocks in pieces:
        draws = jax.random.uniform(jax.random.fold_in(jax.random.fold_in(rng, 6), dim), (blocks,), jnp.float32, smallest / len(pieces), largest / len(pieces))
        loudness = loudness * jnp.repeat(jnp.exp(draws), dims[dim] // blocks).reshape((-1,) + (1,) * (len(dims) - 1 - dim))
    return loudness


def setup_inputs(seed: int = 0, part: int = 0) -> dict:
    arg_keys = jax.random.split(jax.random.key(seed), 10)
    own_keys = jax.random.split(jax.random.fold_in(arg_keys[9], part), 10)
    coords = jnp.clip(24.0 * jax.random.uniform(own_keys[0], (3, ATOMS), jnp.float32) ** block_scale(own_keys[0], (3, ATOMS), ((1, 16),), -0.2, 0.2), 0.0, 24.0)
    atom_types = set_ends(jax.random.randint(own_keys[1], (ATOMS,), 0, TYPES), jax.random.fold_in(own_keys[1], 1), 0, TYPES - 1).astype(jnp.int32)
    slot_atom = draw_slot_atom(jax.random.fold_in(jax.random.fold_in(arg_keys[9], part), 71), part)
    block_pairs = draw_block_pairs(jax.random.fold_in(jax.random.fold_in(arg_keys[9], part), 71), part)
    pair_count = draw_pair_count(jax.random.fold_in(jax.random.fold_in(arg_keys[9], part), 71), part)
    exclusion = set_ends(jax.random.randint(own_keys[5], (BLOCKS, BLOCK // 2), 0, 2**30), jax.random.fold_in(own_keys[5], 1), 0, (2**30) - 1).astype(jnp.int32)
    sigma_type = jnp.clip(jax.random.uniform(arg_keys[6], (TYPES,), jnp.float32, 2.5, 4.0), 2.5, 4.0)
    well_type = jnp.clip(jax.random.uniform(arg_keys[7], (TYPES,), jnp.float32, 0.1, 0.5), 0.1, 0.5)
    charge_type = jnp.clip(jax.random.uniform(arg_keys[8], (TYPES,), jnp.float32, -0.8, 0.8), -0.8, 0.8)
    return dict(coords=coords, atom_types=atom_types, slot_atom=slot_atom, block_pairs=block_pairs, pair_count=pair_count, exclusion=exclusion, sigma_type=sigma_type, well_type=well_type, charge_type=charge_type)


coulomb = 83.0159
cutoff_sq = 144.0

def tile_forces(first_places, first_params, second_places, second_params, weight):
    offset = first_places[..., :, :, None] - second_places[..., :, None, :]
    dist_sq = lax.optimization_barrier(jnp.sum(offset * offset, axis=-3))
    radius = 0.5 * (first_params[..., 0, :, None] + second_params[..., 0, None, :])
    radius_sq = radius * radius
    depth_ij = first_params[..., 1, :, None] * second_params[..., 1, None, :]
    charges = first_params[..., 2, :, None] * second_params[..., 2, None, :]
    inverse = 1.0 / (dist_sq + radius_sq)
    root_inv = jnp.sqrt(inverse)
    ratio_sq = radius_sq * inverse
    attract = ratio_sq * ratio_sq * ratio_sq
    repulse = attract * attract
    energy = 4.0 * depth_ij * (repulse - attract) + coulomb * charges * root_inv
    derivative = 4.0 * depth_ij * (3.0 * attract - 6.0 * repulse) * inverse - 0.5 * coulomb * charges * root_inv * inverse
    window = jnp.maximum(1.0 - dist_sq / cutoff_sq, 0.0)
    strength = -2.0 * (derivative * window * window - energy * 2.0 * window / cutoff_sq) * weight
    pushed = strength[..., None, :, :] * offset
    return (lax.optimization_barrier(jnp.sum(pushed, axis=-1)), -lax.optimization_barrier(jnp.sum(pushed, axis=-2)))

def pair_weight(packed, block_size):
    atom_index = jnp.arange(block_size, dtype=jnp.int32)
    atom_gap = atom_index[None, :] - atom_index[:, None]
    bit_place = (atom_index[:, None] % 2 * 15 + jnp.clip(atom_gap - 1, 0, 14)).astype(jnp.int32)
    picked = packed[:, atom_index // 2]
    bit_value = jnp.bitwise_and(jnp.right_shift(picked[:, :, None], bit_place[None, :, :]), 1)
    banned = (bit_value == 1) & (atom_gap >= 1) & (atom_gap <= 15)
    allowed = (atom_gap >= 1) & jnp.logical_not(banned)
    return allowed.astype(jnp.float32)

def reference(coords, atom_types, slot_atom, block_pairs, pair_count, exclusion, sigma_type, well_type, charge_type):
    device_base = jnp.arange(ATOMS, dtype=jnp.int32) // ATOM_DEV * ATOM_DEV
    atom_order = (device_base + slot_atom).astype(jnp.int32)
    places = coords[:, atom_order]
    slot_kinds = atom_types[atom_order]
    params = jnp.stack([sigma_type[slot_kinds], well_type[slot_kinds], charge_type[slot_kinds]])
    place_blocks = places.reshape(3, BLOCKS, BLOCK).transpose(1, 0, 2)
    param_blocks = params.reshape(3, BLOCKS, BLOCK).transpose(1, 0, 2)
    slot_index = jnp.arange(PAIRS_DEV, dtype=jnp.int32)

    def one_device(forces, device):
        row_place = device // N_COL
        col_place = device % N_COL
        own_blocks = device * BLK_DEV + jnp.arange(BLK_DEV, dtype=jnp.int32)
        own_words = lax.dynamic_slice_in_dim(exclusion, device * BLK_DEV, BLK_DEV, 0)
        weight = pair_weight(own_words, BLOCK)
        own_places = place_blocks[own_blocks]
        own_params = param_blocks[own_blocks]
        on_first, on_second = tile_forces(own_places, own_params, own_places, own_params, weight)
        forces = forces.at[own_blocks].add(on_first + on_second)
        pair_rows = lax.dynamic_slice_in_dim(block_pairs, device * PAIRS_DEV, PAIRS_DEV, 1)
        first_blocks = (row_place * ROW_BLOCKS + pair_rows[0]).astype(jnp.int32)
        second_blocks = ((pair_rows[1] // BLK_DEV * N_COL + col_place) * BLK_DEV + pair_rows[1] % BLK_DEV).astype(jnp.int32)
        live_mask = (slot_index < pair_count[device]).astype(jnp.float32)
        on_first, on_second = tile_forces(place_blocks[first_blocks], param_blocks[first_blocks], place_blocks[second_blocks], param_blocks[second_blocks], live_mask[:, None, None])
        forces = forces.at[first_blocks].add(on_first)
        forces = forces.at[second_blocks].add(on_second)
        return (forces, None)
    forces, unused = lax.scan(one_device, jnp.zeros((BLOCKS, 3, BLOCK), jnp.float32), jnp.arange(N_ROW * N_COL, dtype=jnp.int32))
    flat = forces.transpose(1, 0, 2).reshape(3, ATOMS)
    return jnp.zeros((3, ATOMS), jnp.float32).at[:, atom_order].set(flat)
```

```python
import functools

import jax
import jax.numpy as jnp
from jax import lax
from jax.experimental import pallas as pl
from jax.experimental.pallas import tpu as pltpu
from jax.sharding import PartitionSpec as P

COULOMB = 83.0159
CUTOFF_SQ = 144.0
CENTER = 12.0
LANES = 128
BLOCKS = 8
ROWS = 40
UNROLL = 4
MESH = pl.DeviceIdType.MESH


def lane_gather(table, lanes):
    return jnp.take_along_axis(table, lanes, axis=1, mode="promise_in_bounds")


def meet_peers(n_row, n_col):
    row, col = lax.axis_index("row"), lax.axis_index("col")
    barrier = pltpu.get_barrier_semaphore()
    for k in range(1, n_row):
        pl.semaphore_signal(
            barrier, inc=1, device_id={"row": lax.rem(row + k, n_row)}, device_id_type=MESH
        )
    for k in range(1, n_col):
        pl.semaphore_signal(
            barrier, inc=1, device_id={"col": lax.rem(col + k, n_col)}, device_id_type=MESH
        )
    pl.semaphore_wait(barrier, n_row - 1 + n_col - 1)


def exchange_kernel(
    n_row, n_col, coords_ref, types_ref, slot_ref, pairs_ref, count_ref,
    all_ref, meta_ref, send_sem, recv_sem, pass_send, pass_recv,
):
    row, col = lax.axis_index("row"), lax.axis_index("col")
    slot = slot_ref[...]
    lane, chunk = slot & (LANES - 1), slot >> 7
    mine = row * n_col + col
    kinds = types_ref[...].astype(jnp.float32)
    for comp in range(4):
        total = jnp.zeros((BLOCKS, LANES), jnp.float32)
        for r in range(BLOCKS):
            if comp < 3:
                source = coords_ref[comp : comp + 1, r * LANES : (r + 1) * LANES] - CENTER
            else:
                source = kinds[r : r + 1]
            source = jnp.broadcast_to(source, (BLOCKS, LANES))
            total = jnp.where(chunk == r, lane_gather(source, lane), total)
        all_ref[mine, comp * BLOCKS : (comp + 1) * BLOCKS, :] = total
    pairs = pairs_ref[...].astype(jnp.float32)
    count = jnp.broadcast_to(count_ref[...].astype(jnp.float32), (1, LANES))
    all_ref[mine, 32:40, :] = jnp.concatenate(
        [pairs, count, jnp.zeros((5, LANES), jnp.float32)], axis=0
    )

    meet_peers(n_row, n_col)

    def copy(slot_index, target, sems):
        return pltpu.make_async_remote_copy(
            src_ref=all_ref.at[slot_index],
            dst_ref=all_ref.at[slot_index],
            send_sem=sems[0],
            recv_sem=sems[1],
            device_id=target,
            device_id_type=MESH,
        )

    sends, passes = [], []
    for k in range(1, n_row):
        there = copy(mine, {"row": lax.rem(row + k, n_row)}, (send_sem.at[k], recv_sem.at[k]))
        there.start()
        sends.append(there)
    for k in range(n_row):
        from_row = lax.rem(row + n_row - k, n_row)
        if k:
            copy(
                from_row * n_col + col, {"row": from_row}, (send_sem.at[k], recv_sem.at[k])
            ).wait_recv()
        for j in range(1, n_col):
            on = copy(
                from_row * n_col + col,
                {"col": lax.rem(col + j, n_col)},
                (pass_send.at[k, j], pass_recv.at[k, j]),
            )
            on.start()
            passes.append(on)
    for k in range(n_row):
        from_row = lax.rem(row + n_row - k, n_row)
        for j in range(1, n_col):
            from_col = lax.rem(col + n_col - j, n_col)
            copy(
                from_row * n_col + from_col,
                {"col": from_col},
                (pass_send.at[k, j], pass_recv.at[k, j]),
            ).wait_recv()
    for there in sends + passes:
        there.wait_send()
    meta_ref[...] = all_ref[:, 32:40, :].astype(jnp.int32)


def split(value):
    high = value.astype(jnp.bfloat16).astype(jnp.float32)
    rest = value - high
    mid = rest.astype(jnp.bfloat16).astype(jnp.float32)
    return high, mid, rest - mid


def row_mask(*rows):
    index = lax.broadcasted_iota(jnp.int32, (8, LANES), 0)
    hit = index == rows[0]
    for r in rows[1:]:
        hit = hit | (index == r)
    return hit


def product_scale(weight):
    index = lax.broadcasted_iota(jnp.int32, (8, LANES), 0)
    well_scale = (4.0 * 12.0 / (CUTOFF_SQ * CUTOFF_SQ)) * weight
    charge_scale = (COULOMB / (CUTOFF_SQ * CUTOFF_SQ)) * weight
    return jnp.where(index == 6, well_scale, jnp.where(index == 7, charge_scale, 1.0))


def load_block(all_ref, table, device, block):
    x = all_ref[pl.ds(device * ROWS + block, 1), :]
    y = all_ref[pl.ds(device * ROWS + block + 8, 1), :]
    z = all_ref[pl.ds(device * ROWS + block + 16, 1), :]
    kind = all_ref[pl.ds(device * ROWS + block + 24, 1), :].astype(jnp.int32)
    params = lane_gather(table, jnp.broadcast_to(kind, (8, LANES)))
    index = lax.broadcasted_iota(jnp.int32, (8, LANES), 0)
    norm = x * x + y * y + z * z
    value = jnp.where(index == 0, x, params)
    value = jnp.where(index == 1, y, value)
    value = jnp.where(index == 2, z, value)
    value = jnp.where(index == 3, norm, value)
    return jnp.where(index == 4, 1.0, value)


def left_side(pieces):
    high, mid, low = pieces
    return jnp.concatenate([high, high, mid, mid, high, low], axis=0)


def right_side(pieces):
    index = lax.broadcasted_iota(jnp.int32, (8, LANES), 0)
    high, mid, low = pieces
    parts = []
    for piece in (high, mid, low):
        one = 1.0 if piece is high else 0.0
        for_q = jnp.where(index < 3, -2.0 * piece, 0.0)
        for_q = jnp.where(index == 3, one, for_q)
        for_q = jnp.where(index == 4, jnp.broadcast_to(piece[3:4], (8, LANES)), for_q)
        for_s = jnp.where(index == 5, one, 0.0)
        for_s = jnp.where(index == 4, jnp.broadcast_to(piece[5:6], (8, LANES)), for_s)
        for_well = jnp.where(index == 6, piece, 0.0)
        for_charge = jnp.where(index == 7, piece, 0.0)
        parts.append(jnp.concatenate([for_q, for_s, for_well, for_charge], axis=1))
    high, mid, low = parts
    return jnp.concatenate([high, mid, high, mid, low, high], axis=0)


def pair_strength(left, right, allowed=None):
    both = jnp.dot(
        left.T.astype(jnp.bfloat16), right.astype(jnp.bfloat16),
        preferred_element_type=jnp.float32,
    )
    q, s = both[:, :LANES], both[:, LANES : 2 * LANES]
    well, charge = both[:, 2 * LANES : 3 * LANES], both[:, 3 * LANES :]
    s_sq = s * s
    root = lax.rsqrt(q + s_sq)
    h = root * root
    ratio = s_sq * h
    u = ratio * ratio * ratio
    w = jnp.maximum(CUTOFF_SQ - q, 0.0)
    t = h * w + (1.0 / 3.0)
    near = (well * u) * ((u - 0.5) * t - (1.0 / 6.0))
    far = (charge * root) * (t + (11.0 / 3.0))
    g = (near + far) * w
    if allowed is not None:
        g = jnp.where(allowed, g, 0.0)
    high = g.astype(jnp.bfloat16)
    low = (g - high.astype(jnp.float32)).astype(jnp.bfloat16)
    return high, low


def both_sums(first, second, high, low):
    transposed = (((1,), (1,)), ((), ()))
    on_first = lax.dot_general(
        second, high, transposed, preferred_element_type=jnp.float32
    ) + lax.dot_general(second, low, transposed, preferred_element_type=jnp.float32)
    on_second = jnp.dot(first, high, preferred_element_type=jnp.float32) + jnp.dot(
        first, low, preferred_element_type=jnp.float32
    )
    return on_first, on_second


def force_kernel(
    n_row, n_col, place_ref, meta_ref, all_ref, excl_ref, sigma_ref, well_ref, charge_ref,
    slot_ref, force_ref, inv_ref, sums_ref, first_list, second_list,
):
    mine = place_ref[0]
    n_dev = n_row * n_col

    table = jnp.concatenate(
        [
            jnp.zeros((5, LANES), jnp.float32),
            0.5 * sigma_ref[...],
            well_ref[...],
            charge_ref[...],
        ],
        axis=0,
    )

    lane_id = lax.broadcasted_iota(jnp.int32, (16, LANES), 1)
    row_id = lax.broadcasted_iota(jnp.int32, (16, LANES), 0)
    atom_id = lax.broadcasted_iota(jnp.int32, (LANES, LANES), 0)
    slot = slot_ref[...]
    for a in range(BLOCKS):
        found = jnp.zeros((16, LANES), jnp.float32)
        for b in range(BLOCKS):
            hit = jnp.where(
                jnp.broadcast_to(slot[b : b + 1], (LANES, LANES)) == atom_id + a * LANES, 1.0, 0.0
            ).astype(jnp.bfloat16)
            names = jnp.where(row_id == 0, lane_id.astype(jnp.float32), float(b))
            found += lax.dot_general(
                names.astype(jnp.bfloat16), hit, (((1,), (1,)), ((), ())),
                preferred_element_type=jnp.float32,
            )
        whole = found[0:1] + LANES * found[1:2]
        inv_ref[a : a + 1, :] = whole.astype(jnp.int32)

    def clear(n, _):
        sums_ref[pl.ds(n * 128, 128), :] = jnp.zeros((128, LANES), jnp.float32)
        return 0

    lax.fori_loop(0, n_dev, clear, 0)

    total = lax.fori_loop(0, n_dev, lambda n, t: t + meta_ref[n, 2, 0], 0)
    start = mine * total // n_dev
    stop = (mine + 1) * total // n_dev

    def list_device(n, before):
        count = meta_ref[n, 2, 0]
        row, col = n // n_col, n % n_col

        def list_pair(s, _):
            p, q = meta_ref[n, 0, s], meta_ref[n, 1, s]
            at = before + s - start
            first_list[at] = row * (BLOCKS * n_col) + p
            second_list[at] = ((q >> 3) * n_col + col) * BLOCKS + (q & 7)
            return 0

        low = jnp.maximum(start - before, 0)
        high = jnp.minimum(count, stop - before)
        lax.fori_loop(low, high, list_pair, 0)
        return before + count

    lax.fori_loop(0, n_dev, list_device, 0)
    for extra in range(UNROLL):
        first_list[stop - start + extra] = 0
        second_list[stop - start + extra] = 0

    def add_tiles(step, _):
        found = []
        for extra in range(UNROLL):
            at = step * UNROLL + extra
            a, b = first_list[at], second_list[at]
            weight = (at < stop - start).astype(jnp.float32)
            first = split(load_block(all_ref, table, a >> 3, a & 7))
            second = split(load_block(all_ref, table, b >> 3, b & 7) * product_scale(weight))
            high, low = pair_strength(left_side(first), right_side(second))
            names = [
                jnp.concatenate(pieces[:2], axis=0).astype(jnp.bfloat16)
                for pieces in (first, second)
            ]
            found.append((a, b) + both_sums(names[0], names[1], high, low))
        for a, b, on_first, on_second in found:
            sums_ref[pl.ds(a * 16, 16), :] += on_first
            sums_ref[pl.ds(b * 16, 16), :] += on_second
        return 0

    lax.fori_loop(0, (stop - start + UNROLL - 1) // UNROLL, add_tiles, 0)

    place_i = lax.broadcasted_iota(jnp.int32, (LANES, LANES), 0)
    place_j = lax.broadcasted_iota(jnp.int32, (LANES, LANES), 1)
    gap = place_j - place_i
    bit = (place_i & 1) * 15 + jnp.clip(gap - 1, 0, 14)
    excl = excl_ref[...]
    half_i = lax.broadcasted_iota(jnp.int32, (LANES, 64), 0) >> 1
    half_k = lax.broadcasted_iota(jnp.int32, (LANES, 64), 1)
    pick = half_i == half_k
    for b in range(BLOCKS):
        words = jnp.broadcast_to(excl[b : b + 1], (LANES, 64))
        word = jnp.sum(jnp.where(pick, words >> 15, 0).astype(jnp.float32), axis=1, keepdims=True)
        word_low = jnp.sum(
            jnp.where(pick, words & 32767, 0).astype(jnp.float32), axis=1, keepdims=True
        )
        odd = lax.broadcasted_iota(jnp.int32, (LANES, 1), 0) & 1
        mine15 = jnp.where(odd == 1, word, word_low).astype(jnp.int32)
        bits = (jnp.broadcast_to(mine15, (LANES, LANES)) >> jnp.clip(gap - 1, 0, 14)) & 1
        allowed = (gap >= 1) & ((gap > 15) | (bits == 0))
        value = load_block(all_ref, table, mine, b)
        pieces = split(value)
        right = right_side(split(value * product_scale(1.0)))
        high, low = pair_strength(left_side(pieces), right, allowed)
        names = jnp.concatenate(pieces[:2], axis=0).astype(jnp.bfloat16)
        on_first, on_second = both_sums(names, names, high, low)
        at = pl.ds((mine * BLOCKS + b) * 16, 16)
        sums_ref[at, :] += on_first + on_second

    def finish(n, _):
        def rows(r):
            return sums_ref[pl.ds(n * 128 + r, BLOCKS, stride=16), :]

        g_sum = rows(4)
        for comp in range(3):
            x = all_ref[pl.ds(n * ROWS + comp * BLOCKS, BLOCKS), :]
            force_ref[n, comp * BLOCKS : (comp + 1) * BLOCKS, :] = (
                x * g_sum - rows(comp) - rows(comp + 8)
            )
        return 0

    lax.fori_loop(0, n_dev, finish, 0)


def return_kernel(
    n_row, n_col, force_ref, inv_ref, out_ref,
    core_buf, send_buf, row_buf, core_send, core_recv, row_send, row_recv,
):
    row, col = lax.axis_index("row"), lax.axis_index("col")
    meet_peers(n_row, n_col)
    sends = []
    order = list(range(1, n_row)) + [0]
    for k in order:
        to_row = lax.rem(row + k, n_row)
        for j in range(1, n_col):
            to_col = lax.rem(col + j, n_col)
            there = pltpu.make_async_remote_copy(
                src_ref=force_ref.at[to_row * n_col + to_col],
                dst_ref=core_buf.at[k, j],
                send_sem=core_send.at[k, j],
                recv_sem=core_recv.at[k, j],
                device_id={"col": to_col},
                device_id_type=MESH,
            )
            there.start()
            sends.append(there)
    arrive = []
    own = None
    at = 0
    for k in order:
        to_row = lax.rem(row + k, n_row)
        part = force_ref[to_row * n_col + col]
        for j in range(1, n_col):
            sends[at].wait_recv()
            at += 1
            part = part + core_buf[k, j]
        if k == 0:
            own = part
        else:
            send_buf[k] = part
            there = pltpu.make_async_remote_copy(
                src_ref=send_buf.at[k],
                dst_ref=row_buf.at[k],
                send_sem=row_send.at[k],
                recv_sem=row_recv.at[k],
                device_id={"row": to_row},
                device_id_type=MESH,
            )
            there.start()
            arrive.append(there)
    for k in range(1, n_row):
        arrive[k - 1].wait_recv()
        own = own + row_buf[k]
    for there in sends + arrive:
        there.wait_send()
    inverse = inv_ref[...]
    lane, chunk = inverse & (LANES - 1), inverse >> 7
    for comp in range(3):
        total = jnp.zeros((BLOCKS, LANES), jnp.float32)
        for r in range(BLOCKS):
            at = comp * BLOCKS + r
            source = jnp.broadcast_to(own[at : at + 1], (BLOCKS, LANES))
            total = jnp.where(chunk == r, lane_gather(source, lane), total)
        for r in range(BLOCKS):
            out_ref[comp : comp + 1, r * LANES : (r + 1) * LANES] = total[r : r + 1]


def body(n_row, n_col, coords, atom_types, slot_atom, block_pairs, pair_count, exclusion,
         sigma_type, well_type, charge_type):
    n_dev = n_row * n_col
    slots = slot_atom.reshape(BLOCKS, LANES)
    vmem = pl.BlockSpec(memory_space=pltpu.VMEM)
    smem = pl.BlockSpec(memory_space=pltpu.SMEM)
    dma = pltpu.SemaphoreType.DMA
    gathered, meta = pl.pallas_call(
        functools.partial(exchange_kernel, n_row, n_col),
        out_shape=(
            jax.ShapeDtypeStruct((n_dev, ROWS, LANES), jnp.float32),
            jax.ShapeDtypeStruct((n_dev, 8, LANES), jnp.int32),
        ),
        in_specs=[vmem] * 5,
        out_specs=(vmem, vmem),
        scratch_shapes=[
            dma((n_row,)), dma((n_row,)), dma((n_row, n_col)), dma((n_row, n_col)),
        ],
        compiler_params=pltpu.CompilerParams(
            collective_id=0, has_side_effects=True, vmem_limit_bytes=32 << 20
        ),
        name="exchange",
    )(coords, atom_types.reshape(BLOCKS, LANES), slots, block_pairs, pair_count.reshape(1, 1))
    place = (lax.axis_index("row") * n_col + lax.axis_index("col")).reshape(1)
    most = block_pairs.shape[1]
    force, inverse = pl.pallas_call(
        functools.partial(force_kernel, n_row, n_col),
        out_shape=(
            jax.ShapeDtypeStruct((n_dev, 24, LANES), jnp.float32),
            jax.ShapeDtypeStruct((BLOCKS, LANES), jnp.int32),
        ),
        in_specs=[smem, smem] + [vmem] * 6,
        out_specs=(vmem, vmem),
        scratch_shapes=[
            pltpu.VMEM((n_dev * 128, LANES), jnp.float32),
            pltpu.SMEM((most + 1 + UNROLL,), jnp.int32),
            pltpu.SMEM((most + 1 + UNROLL,), jnp.int32),
        ],
        compiler_params=pltpu.CompilerParams(vmem_limit_bytes=48 << 20),
        name="pair_forces",
    )(
        place, meta, gathered.reshape(n_dev * ROWS, LANES), exclusion,
        sigma_type.reshape(1, LANES), well_type.reshape(1, LANES),
        charge_type.reshape(1, LANES), slots,
    )
    return pl.pallas_call(
        functools.partial(return_kernel, n_row, n_col),
        out_shape=jax.ShapeDtypeStruct(coords.shape, jnp.float32),
        in_specs=[vmem, vmem],
        out_specs=vmem,
        scratch_shapes=[
            pltpu.VMEM((n_row, n_col, 24, LANES), jnp.float32),
            pltpu.VMEM((n_row, 24, LANES), jnp.float32),
            pltpu.VMEM((n_row, 24, LANES), jnp.float32),
            dma((n_row, n_col)), dma((n_row, n_col)), dma((n_row,)), dma((n_row,)),
        ],
        compiler_params=pltpu.CompilerParams(
            collective_id=1, has_side_effects=True, vmem_limit_bytes=32 << 20
        ),
        name="return_forces",
    )(force, inverse)


def solution(mesh):
    every = ("groups", "row", "col")
    return jax.shard_map(
        functools.partial(body, mesh.shape["row"], mesh.shape["col"]),
        mesh=mesh,
        in_specs=(
            P(None, every), P(every), P(every), P(None, every), P(every), P(every, None),
            P(), P(), P(),
        ),
        out_specs=P(None, every),
        check_vma=False,
    )
```

```python
import functools

import jax
import jax.numpy as jnp
from jax import lax
from jax.experimental import pallas as pl
from jax.experimental.pallas import tpu as pltpu
from jax.sharding import PartitionSpec as P

COULOMB = 83.0159
CUTOFF_SQ = 144.0
CENTER = 12.0
LANES = 128
BLOCKS = 8
ROWS = 40
UNROLL = 8
MESH = pl.DeviceIdType.MESH


def lane_gather(table, lanes):
    return jnp.take_along_axis(table, lanes, axis=1, mode="promise_in_bounds")


def greet_peers(n_row, n_col):
    row, col = lax.axis_index("row"), lax.axis_index("col")
    barrier = pltpu.get_barrier_semaphore()
    for k in range(1, n_row):
        pl.semaphore_signal(
            barrier, inc=1, device_id={"row": lax.rem(row + k, n_row)}, device_id_type=MESH
        )
    for k in range(1, n_col):
        pl.semaphore_signal(
            barrier, inc=1, device_id={"col": lax.rem(col + k, n_col)}, device_id_type=MESH
        )
    return barrier


def exchange_kernel(
    n_row, n_col, coords_ref, types_ref, slot_ref, pairs_ref, count_ref, excl_ref,
    sigma_ref, well_ref, charge_ref, all_ref, meta_ref, own_ref, inv_ref, send_sem, recv_sem, pass_send, pass_recv,
):
    row, col = lax.axis_index("row"), lax.axis_index("col")
    barrier = greet_peers(n_row, n_col)
    slot = slot_ref[...]
    own = []
    lane, chunk = slot & (LANES - 1), slot >> 7
    mine = row * n_col + col
    kinds = types_ref[...].astype(jnp.float32)
    for comp in range(4):
        total = jnp.zeros((BLOCKS, LANES), jnp.float32)
        for r in range(BLOCKS):
            if comp < 3:
                source = coords_ref[comp : comp + 1, r * LANES : (r + 1) * LANES] - CENTER
            else:
                source = kinds[r : r + 1]
            source = jnp.broadcast_to(source, (BLOCKS, LANES))
            total = jnp.where(chunk == r, lane_gather(source, lane), total)
        all_ref[mine, comp * BLOCKS : (comp + 1) * BLOCKS, :] = total
        own.append(total)
    pairs = pairs_ref[...].astype(jnp.float32)
    count = jnp.broadcast_to(count_ref[...].astype(jnp.float32), (1, LANES))
    all_ref[mine, 32:40, :] = jnp.concatenate(
        [pairs, count, jnp.zeros((5, LANES), jnp.float32)], axis=0
    )

    pl.semaphore_wait(barrier, n_row - 1 + n_col - 1)

    def copy(slot_index, target, sems):
        return pltpu.make_async_remote_copy(
            src_ref=all_ref.at[slot_index],
            dst_ref=all_ref.at[slot_index],
            send_sem=sems[0],
            recv_sem=sems[1],
            device_id=target,
            device_id_type=MESH,
        )

    sends, passes = [], []
    for k in range(1, n_row):
        there = copy(mine, {"row": lax.rem(row + k, n_row)}, (send_sem.at[k], recv_sem.at[k]))
        there.start()
        sends.append(there)
    for k in range(n_row):
        from_row = lax.rem(row + n_row - k, n_row)
        if k == 1:
            own_pairs(own, excl_ref, type_rows(sigma_ref, well_ref, charge_ref), own_ref)
        if k:
            copy(
                from_row * n_col + col, {"row": from_row}, (send_sem.at[k], recv_sem.at[k])
            ).wait_recv()
        for j in range(1, n_col):
            on = copy(
                from_row * n_col + col,
                {"col": lax.rem(col + j, n_col)},
                (pass_send.at[k, j], pass_recv.at[k, j]),
            )
            on.start()
            passes.append(on)
    invert(slot, inv_ref)
    for k in range(n_row):
        from_row = lax.rem(row + n_row - k, n_row)
        for j in range(1, n_col):
            from_col = lax.rem(col + n_col - j, n_col)
            copy(
                from_row * n_col + from_col,
                {"col": from_col},
                (pass_send.at[k, j], pass_recv.at[k, j]),
            ).wait_recv()
    for there in sends + passes:
        there.wait_send()
    meta_ref[...] = all_ref[:, 32:40, :].astype(jnp.int32)


def split(value):
    high = value.astype(jnp.bfloat16).astype(jnp.float32)
    rest = value - high
    mid = rest.astype(jnp.bfloat16).astype(jnp.float32)
    return high, mid, rest - mid


def row_mask(*rows):
    index = lax.broadcasted_iota(jnp.int32, (8, LANES), 0)
    hit = index == rows[0]
    for r in rows[1:]:
        hit = hit | (index == r)
    return hit


def product_scale(weight):
    index = lax.broadcasted_iota(jnp.int32, (8, LANES), 0)
    well_scale = (4.0 * 12.0 / (CUTOFF_SQ * CUTOFF_SQ)) * weight
    charge_scale = (COULOMB / (CUTOFF_SQ * CUTOFF_SQ)) * weight
    return jnp.where(index == 6, well_scale, jnp.where(index == 7, charge_scale, 1.0))


def type_rows(sigma_ref, well_ref, charge_ref):
    return jnp.concatenate(
        [
            jnp.zeros((5, LANES), jnp.float32),
            0.5 * sigma_ref[...],
            well_ref[...],
            charge_ref[...],
        ],
        axis=0,
    )


def load_block(all_ref, table, device, block):
    return block_rows(
        [all_ref[pl.ds(device * ROWS + block + 8 * comp, 1), :] for comp in range(4)], table
    )


def block_rows(parts, table):
    x, y, z, kind = parts
    kind = kind.astype(jnp.int32)
    params = lane_gather(table, jnp.broadcast_to(kind, (8, LANES)))
    index = lax.broadcasted_iota(jnp.int32, (8, LANES), 0)
    norm = x * x + y * y + z * z
    value = jnp.where(index == 0, x, params)
    value = jnp.where(index == 1, y, value)
    value = jnp.where(index == 2, z, value)
    value = jnp.where(index == 3, norm, value)
    return jnp.where(index == 4, 1.0, value)


def left_side(pieces):
    high, mid, low = pieces
    return jnp.concatenate([high, high, mid, mid, high, low], axis=0)


def right_side(pieces):
    index = lax.broadcasted_iota(jnp.int32, (8, LANES), 0)
    high, mid, low = pieces
    parts = []
    for piece in (high, mid, low):
        one = 1.0 if piece is high else 0.0
        for_q = jnp.where(index < 3, -2.0 * piece, 0.0)
        for_q = jnp.where(index == 3, one, for_q)
        for_q = jnp.where(index == 4, jnp.broadcast_to(piece[3:4], (8, LANES)), for_q)
        for_s = jnp.where(index == 5, one, 0.0)
        for_s = jnp.where(index == 4, jnp.broadcast_to(piece[5:6], (8, LANES)), for_s)
        for_well = jnp.where(index == 6, piece, 0.0)
        for_charge = jnp.where(index == 7, piece, 0.0)
        parts.append(jnp.concatenate([for_q, for_s, for_well, for_charge], axis=1))
    high, mid, low = parts
    return jnp.concatenate([high, mid, high, mid, low, high], axis=0)


def pair_strength(left, right, allowed=None):
    both = jnp.dot(
        left.T.astype(jnp.bfloat16), right.astype(jnp.bfloat16),
        preferred_element_type=jnp.float32,
    )
    q, s = both[:, :LANES], both[:, LANES : 2 * LANES]
    well, charge = both[:, 2 * LANES : 3 * LANES], both[:, 3 * LANES :]
    s_sq = s * s
    root = lax.rsqrt(q + s_sq)
    h = root * root
    ratio = s_sq * h
    u = ratio * ratio * ratio
    w = jnp.maximum(CUTOFF_SQ - q, 0.0)
    t = h * w + (1.0 / 3.0)
    near = (well * u) * ((u - 0.5) * t - (1.0 / 6.0))
    far = (charge * root) * (t + (11.0 / 3.0))
    g = (near + far) * w
    if allowed is not None:
        g = jnp.where(allowed, g, 0.0)
    high = g.astype(jnp.bfloat16)
    low = (g - high.astype(jnp.float32)).astype(jnp.bfloat16)
    return high, low


def both_sums(first, second, high, low):
    high_low = jnp.concatenate([high, low], axis=1)
    on_first = lax.dot_general(
        jnp.concatenate([second, second], axis=1), high_low, (((1,), (1,)), ((), ())),
        preferred_element_type=jnp.float32,
    )
    on_second = jnp.dot(
        jnp.concatenate([first, first], axis=1), jnp.concatenate([high, low], axis=0),
        preferred_element_type=jnp.float32,
    )
    return on_first, on_second


def invert(slot, inv_ref):
    lane_id = lax.broadcasted_iota(jnp.int32, (16, LANES), 1)
    row_id = lax.broadcasted_iota(jnp.int32, (16, LANES), 0)
    atom_id = lax.broadcasted_iota(jnp.int32, (LANES, LANES), 0)
    for a in range(BLOCKS):
        found = jnp.zeros((16, LANES), jnp.float32)
        for b in range(BLOCKS):
            hit = jnp.where(
                jnp.broadcast_to(slot[b : b + 1], (LANES, LANES)) == atom_id + a * LANES, 1.0, 0.0
            ).astype(jnp.bfloat16)
            names = jnp.where(row_id == 0, lane_id.astype(jnp.float32), float(b))
            found += lax.dot_general(
                names.astype(jnp.bfloat16), hit, (((1,), (1,)), ((), ())),
                preferred_element_type=jnp.float32,
            )
        whole = found[0:1] + LANES * found[1:2]
        inv_ref[a : a + 1, :] = whole.astype(jnp.int32)


def own_pairs(own, excl_ref, table, own_ref):
    place_i = lax.broadcasted_iota(jnp.int32, (LANES, LANES), 0)
    place_j = lax.broadcasted_iota(jnp.int32, (LANES, LANES), 1)
    gap = place_j - place_i
    excl = excl_ref[...]
    half_i = lax.broadcasted_iota(jnp.int32, (LANES, 64), 0) >> 1
    half_k = lax.broadcasted_iota(jnp.int32, (LANES, 64), 1)
    pick = half_i == half_k
    for b in range(BLOCKS):
        words = jnp.broadcast_to(excl[b : b + 1], (LANES, 64))
        word = jnp.sum(jnp.where(pick, words >> 15, 0).astype(jnp.float32), axis=1, keepdims=True)
        word_low = jnp.sum(
            jnp.where(pick, words & 32767, 0).astype(jnp.float32), axis=1, keepdims=True
        )
        odd = lax.broadcasted_iota(jnp.int32, (LANES, 1), 0) & 1
        mine15 = jnp.where(odd == 1, word, word_low).astype(jnp.int32)
        bits = (jnp.broadcast_to(mine15, (LANES, LANES)) >> jnp.clip(gap - 1, 0, 14)) & 1
        allowed = (gap >= 1) & ((gap > 15) | (bits == 0))
        value = block_rows([part[b : b + 1] for part in own], table)
        pieces = split(value)
        right = right_side(split(value * product_scale(1.0)))
        high, low = pair_strength(left_side(pieces), right, allowed)
        names = jnp.concatenate(pieces[:2], axis=0).astype(jnp.bfloat16)
        on_first, on_second = both_sums(names, names, high, low)
        own_ref[b * 16 : (b + 1) * 16, :] = on_first + on_second


def force_kernel(
    n_row, n_col, place_ref, meta_ref, all_ref, sigma_ref, well_ref, charge_ref,
    own_ref, force_ref, sums_ref, first_list, second_list,
):
    mine = place_ref[0]
    n_dev = n_row * n_col

    table = type_rows(sigma_ref, well_ref, charge_ref)

    def clear(n, _):
        sums_ref[pl.ds(n * 128, 128), :] = jnp.zeros((128, LANES), jnp.float32)
        return 0

    lax.fori_loop(0, n_dev, clear, 0)
    sums_ref[pl.ds(mine * 128, 128), :] = own_ref[...]

    total = lax.fori_loop(0, n_dev, lambda n, t: t + meta_ref[n, 2, 0], 0)
    start = mine * total // n_dev
    stop = (mine + 1) * total // n_dev

    def list_device(n, before):
        count = meta_ref[n, 2, 0]
        row, col = n // n_col, n % n_col

        def list_pair(s, _):
            p, q = meta_ref[n, 0, s], meta_ref[n, 1, s]
            at = before + s - start
            first_list[at] = row * (BLOCKS * n_col) + p
            second_list[at] = ((q >> 3) * n_col + col) * BLOCKS + (q & 7)
            return 0

        low = jnp.maximum(start - before, 0)
        high = jnp.minimum(count, stop - before)
        lax.fori_loop(low, high, list_pair, 0)
        return before + count

    lax.fori_loop(0, n_dev, list_device, 0)
    for extra in range(UNROLL):
        first_list[stop - start + extra] = 0
        second_list[stop - start + extra] = 0

    def add_tiles(step, _):
        found = []
        for extra in range(UNROLL):
            at = step * UNROLL + extra
            a, b = first_list[at], second_list[at]
            weight = (at < stop - start).astype(jnp.float32)
            first = split(load_block(all_ref, table, a >> 3, a & 7))
            second = split(load_block(all_ref, table, b >> 3, b & 7) * product_scale(weight))
            high, low = pair_strength(left_side(first), right_side(second))
            names = [
                jnp.concatenate(pieces[:2], axis=0).astype(jnp.bfloat16)
                for pieces in (first, second)
            ]
            found.append((a, b) + both_sums(names[0], names[1], high, low))
        for a, b, on_first, on_second in found:
            sums_ref[pl.ds(a * 16, 16), :] += on_first
            sums_ref[pl.ds(b * 16, 16), :] += on_second
        return 0

    lax.fori_loop(0, (stop - start + UNROLL - 1) // UNROLL, add_tiles, 0)

    def finish(n, _):
        def rows(r):
            return sums_ref[pl.ds(n * 128 + r, BLOCKS, stride=16), :]

        g_sum = rows(4)
        for comp in range(3):
            x = all_ref[pl.ds(n * ROWS + comp * BLOCKS, BLOCKS), :]
            force_ref[n, comp * BLOCKS : (comp + 1) * BLOCKS, :] = (
                x * g_sum - rows(comp) - rows(comp + 8)
            )
        return 0

    lax.fori_loop(0, n_dev, finish, 0)


def return_kernel(
    n_row, n_col, force_ref, inv_ref, out_ref,
    core_buf, send_buf, row_buf, core_send, core_recv, row_send, row_recv,
):
    row, col = lax.axis_index("row"), lax.axis_index("col")
    barrier = greet_peers(n_row, n_col)
    pl.semaphore_wait(barrier, n_row - 1 + n_col - 1)
    sends = []
    order = list(range(1, n_row)) + [0]
    for k in order:
        to_row = lax.rem(row + k, n_row)
        for j in range(1, n_col):
            to_col = lax.rem(col + j, n_col)
            there = pltpu.make_async_remote_copy(
                src_ref=force_ref.at[to_row * n_col + to_col],
                dst_ref=core_buf.at[k, j],
                send_sem=core_send.at[k, j],
                recv_sem=core_recv.at[k, j],
                device_id={"col": to_col},
                device_id_type=MESH,
            )
            there.start()
            sends.append(there)
    arrive = []
    own = None
    at = 0
    for k in order:
        to_row = lax.rem(row + k, n_row)
        part = force_ref[to_row * n_col + col]
        for j in range(1, n_col):
            sends[at].wait_recv()
            at += 1
            part = part + core_buf[k, j]
        if k == 0:
            own = part
        else:
            send_buf[k] = part
            there = pltpu.make_async_remote_copy(
                src_ref=send_buf.at[k],
                dst_ref=row_buf.at[k],
                send_sem=row_send.at[k],
                recv_sem=row_recv.at[k],
                device_id={"row": to_row},
                device_id_type=MESH,
            )
            there.start()
            arrive.append(there)
    for k in range(1, n_row):
        arrive[k - 1].wait_recv()
        own = own + row_buf[k]
    for there in sends + arrive:
        there.wait_send()
    inverse = inv_ref[...]
    lane, chunk = inverse & (LANES - 1), inverse >> 7
    for comp in range(3):
        total = jnp.zeros((BLOCKS, LANES), jnp.float32)
        for r in range(BLOCKS):
            at = comp * BLOCKS + r
            source = jnp.broadcast_to(own[at : at + 1], (BLOCKS, LANES))
            total = jnp.where(chunk == r, lane_gather(source, lane), total)
        for r in range(BLOCKS):
            out_ref[comp : comp + 1, r * LANES : (r + 1) * LANES] = total[r : r + 1]


def body(n_row, n_col, coords, atom_types, slot_atom, block_pairs, pair_count, exclusion,
         sigma_type, well_type, charge_type):
    n_dev = n_row * n_col
    slots = slot_atom.reshape(BLOCKS, LANES)
    vmem = pl.BlockSpec(memory_space=pltpu.VMEM)
    smem = pl.BlockSpec(memory_space=pltpu.SMEM)
    dma = pltpu.SemaphoreType.DMA
    tables = [t.reshape(1, LANES) for t in (sigma_type, well_type, charge_type)]
    gathered, meta, own, inverse = pl.pallas_call(
        functools.partial(exchange_kernel, n_row, n_col),
        out_shape=(
            jax.ShapeDtypeStruct((n_dev, ROWS, LANES), jnp.float32),
            jax.ShapeDtypeStruct((n_dev, 8, LANES), jnp.int32),
            jax.ShapeDtypeStruct((BLOCKS * 16, LANES), jnp.float32),
            jax.ShapeDtypeStruct((BLOCKS, LANES), jnp.int32),
        ),
        in_specs=[vmem] * 9,
        out_specs=(vmem,) * 4,
        scratch_shapes=[
            dma((n_row,)), dma((n_row,)), dma((n_row, n_col)), dma((n_row, n_col)),
        ],
        compiler_params=pltpu.CompilerParams(
            collective_id=0, has_side_effects=True, vmem_limit_bytes=32 << 20
        ),
        name="exchange",
    )(coords, atom_types.reshape(BLOCKS, LANES), slots, block_pairs, pair_count.reshape(1, 1),
      exclusion, *tables)
    place = (lax.axis_index("row") * n_col + lax.axis_index("col")).reshape(1)
    most = block_pairs.shape[1]
    force = pl.pallas_call(
        functools.partial(force_kernel, n_row, n_col),
        out_shape=jax.ShapeDtypeStruct((n_dev, 24, LANES), jnp.float32),
        in_specs=[smem, smem] + [vmem] * 5,
        out_specs=vmem,
        scratch_shapes=[
            pltpu.VMEM((n_dev * 128, LANES), jnp.float32),
            pltpu.SMEM((most + 1 + UNROLL,), jnp.int32),
            pltpu.SMEM((most + 1 + UNROLL,), jnp.int32),
        ],
        compiler_params=pltpu.CompilerParams(vmem_limit_bytes=48 << 20),
        name="pair_forces",
    )(
        place, meta, gathered.reshape(n_dev * ROWS, LANES), *tables, own,
    )
    return pl.pallas_call(
        functools.partial(return_kernel, n_row, n_col),
        out_shape=jax.ShapeDtypeStruct(coords.shape, jnp.float32),
        in_specs=[vmem, vmem],
        out_specs=vmem,
        scratch_shapes=[
            pltpu.VMEM((n_row, n_col, 24, LANES), jnp.float32),
            pltpu.VMEM((n_row, 24, LANES), jnp.float32),
            pltpu.VMEM((n_row, 24, LANES), jnp.float32),
            dma((n_row, n_col)), dma((n_row, n_col)), dma((n_row,)), dma((n_row,)),
        ],
        compiler_params=pltpu.CompilerParams(
            collective_id=1, has_side_effects=True, vmem_limit_bytes=32 << 20
        ),
        name="return_forces",
    )(force, inverse)


def solution(mesh):
    every = ("groups", "row", "col")
    return jax.shard_map(
        functools.partial(body, mesh.shape["row"], mesh.shape["col"]),
        mesh=mesh,
        in_specs=(
            P(None, every), P(every), P(every), P(None, every), P(every), P(every, None),
            P(), P(), P(),
        ),
        out_specs=P(None, every),
        check_vma=False,
    )
```

```python
import functools

import jax
import jax.numpy as jnp
from jax import lax
from jax.experimental import pallas as pl
from jax.experimental.pallas import tpu as pltpu
from jax.sharding import PartitionSpec as P

COULOMB = 83.0159
CUTOFF_SQ = 144.0
CENTER = 12.0
LANES = 128
BLOCKS = 8
ROWS = 40
UNROLL = 8
MESH = pl.DeviceIdType.MESH


def lane_gather(table, lanes):
    return jnp.take_along_axis(table, lanes, axis=1, mode="promise_in_bounds")


def greet_peers(n_row, n_col):
    row, col = lax.axis_index("row"), lax.axis_index("col")
    barrier = pltpu.get_barrier_semaphore()
    for k in range(1, n_row):
        pl.semaphore_signal(
            barrier, inc=1, device_id={"row": lax.rem(row + k, n_row)}, device_id_type=MESH
        )
    for k in range(1, n_col):
        pl.semaphore_signal(
            barrier, inc=1, device_id={"col": lax.rem(col + k, n_col)}, device_id_type=MESH
        )
    return barrier


def exchange_kernel(
    n_row, n_col, count_ref, *refs,
):
    inputs, (all_ref, meta_ref, own_ref, inv_ref), local = refs[:8], refs[8:12], refs[12:20]
    load_sem, send_sem, recv_sem, pass_send, pass_recv = refs[20:]
    loads = [
        pltpu.make_async_copy(source, target, load_sem.at[k])
        for k, (source, target) in enumerate(zip(inputs, local))
    ]
    for load in loads:
        load.start()
    coords_ref, types_ref, slot_ref, pairs_ref, excl_ref, sigma_ref, well_ref, charge_ref = local
    row, col = lax.axis_index("row"), lax.axis_index("col")
    barrier = greet_peers(n_row, n_col)
    for load in loads:
        load.wait()
    slot = slot_ref[...]
    own = []
    lane, chunk = slot & (LANES - 1), slot >> 7
    mine = row * n_col + col
    kinds = types_ref[...].astype(jnp.float32)
    for comp in range(4):
        total = jnp.zeros((BLOCKS, LANES), jnp.float32)
        for r in range(BLOCKS):
            if comp < 3:
                source = coords_ref[comp : comp + 1, r * LANES : (r + 1) * LANES] - CENTER
            else:
                source = kinds[r : r + 1]
            source = jnp.broadcast_to(source, (BLOCKS, LANES))
            total = jnp.where(chunk == r, lane_gather(source, lane), total)
        all_ref[mine, comp * BLOCKS : (comp + 1) * BLOCKS, :] = total
        own.append(total)
    pairs = pairs_ref[...].astype(jnp.float32)
    count = jnp.full((1, LANES), count_ref[0], jnp.int32).astype(jnp.float32)
    all_ref[mine, 32:40, :] = jnp.concatenate(
        [pairs, count, jnp.zeros((5, LANES), jnp.float32)], axis=0
    )

    pl.semaphore_wait(barrier, n_row - 1 + n_col - 1)

    def copy(slot_index, target, sems):
        return pltpu.make_async_remote_copy(
            src_ref=all_ref.at[slot_index],
            dst_ref=all_ref.at[slot_index],
            send_sem=sems[0],
            recv_sem=sems[1],
            device_id=target,
            device_id_type=MESH,
        )

    sends, passes = [], []
    for k in range(1, n_row):
        there = copy(mine, {"row": lax.rem(row + k, n_row)}, (send_sem.at[k], recv_sem.at[k]))
        there.start()
        sends.append(there)
    for k in range(n_row):
        from_row = lax.rem(row + n_row - k, n_row)
        if k == 1:
            own_pairs(own, excl_ref, type_rows(sigma_ref, well_ref, charge_ref), own_ref)
        if k:
            copy(
                from_row * n_col + col, {"row": from_row}, (send_sem.at[k], recv_sem.at[k])
            ).wait_recv()
        for j in range(1, n_col):
            on = copy(
                from_row * n_col + col,
                {"col": lax.rem(col + j, n_col)},
                (pass_send.at[k, j], pass_recv.at[k, j]),
            )
            on.start()
            passes.append(on)
    invert(slot, inv_ref)
    for k in range(n_row):
        from_row = lax.rem(row + n_row - k, n_row)
        for j in range(1, n_col):
            from_col = lax.rem(col + n_col - j, n_col)
            copy(
                from_row * n_col + from_col,
                {"col": from_col},
                (pass_send.at[k, j], pass_recv.at[k, j]),
            ).wait_recv()
    for there in sends + passes:
        there.wait_send()
    meta_ref[...] = all_ref[:, 32:40, :].astype(jnp.int32)
    meta_ref[0, 3:4, :] = jnp.full((1, LANES), mine, jnp.int32)


def split(value):
    high = value.astype(jnp.bfloat16).astype(jnp.float32)
    rest = value - high
    mid = rest.astype(jnp.bfloat16).astype(jnp.float32)
    return high, mid, rest - mid


def row_mask(*rows):
    index = lax.broadcasted_iota(jnp.int32, (8, LANES), 0)
    hit = index == rows[0]
    for r in rows[1:]:
        hit = hit | (index == r)
    return hit


def product_scale(weight):
    index = lax.broadcasted_iota(jnp.int32, (8, LANES), 0)
    well_scale = (4.0 * 12.0 / (CUTOFF_SQ * CUTOFF_SQ)) * weight
    charge_scale = (COULOMB / (CUTOFF_SQ * CUTOFF_SQ)) * weight
    return jnp.where(index == 6, well_scale, jnp.where(index == 7, charge_scale, 1.0))


def type_rows(sigma_ref, well_ref, charge_ref):
    return jnp.concatenate(
        [
            jnp.zeros((5, LANES), jnp.float32),
            0.5 * sigma_ref[...],
            well_ref[...],
            charge_ref[...],
        ],
        axis=0,
    )


def load_block(all_ref, table, device, block):
    return block_rows(
        [all_ref[pl.ds(device * ROWS + block + 8 * comp, 1), :] for comp in range(4)], table
    )


def block_rows(parts, table):
    x, y, z, kind = parts
    kind = kind.astype(jnp.int32)
    params = lane_gather(table, jnp.broadcast_to(kind, (8, LANES)))
    index = lax.broadcasted_iota(jnp.int32, (8, LANES), 0)
    norm = x * x + y * y + z * z
    value = jnp.where(index == 0, x, params)
    value = jnp.where(index == 1, y, value)
    value = jnp.where(index == 2, z, value)
    value = jnp.where(index == 3, norm, value)
    return jnp.where(index == 4, 1.0, value)


def left_side(pieces):
    high, mid, low = pieces
    return jnp.concatenate([high, high, mid, mid, high, low], axis=0)


def right_side(pieces):
    index = lax.broadcasted_iota(jnp.int32, (8, LANES), 0)
    high, mid, low = pieces
    parts = []
    for piece in (high, mid, low):
        one = 1.0 if piece is high else 0.0
        for_q = jnp.where(index < 3, -2.0 * piece, 0.0)
        for_q = jnp.where(index == 3, one, for_q)
        for_q = jnp.where(index == 4, jnp.broadcast_to(piece[3:4], (8, LANES)), for_q)
        for_s = jnp.where(index == 5, one, 0.0)
        for_s = jnp.where(index == 4, jnp.broadcast_to(piece[5:6], (8, LANES)), for_s)
        for_well = jnp.where(index == 6, piece, 0.0)
        for_charge = jnp.where(index == 7, piece, 0.0)
        parts.append(jnp.concatenate([for_q, for_s, for_well, for_charge], axis=1))
    high, mid, low = parts
    return jnp.concatenate([high, mid, high, mid, low, high], axis=0)


def pair_strength(left, right, allowed=None):
    both = jnp.dot(
        left.T.astype(jnp.bfloat16), right.astype(jnp.bfloat16),
        preferred_element_type=jnp.float32,
    )
    q, s = both[:, :LANES], both[:, LANES : 2 * LANES]
    well, charge = both[:, 2 * LANES : 3 * LANES], both[:, 3 * LANES :]
    s_sq = s * s
    root = lax.rsqrt(q + s_sq)
    h = root * root
    ratio = s_sq * h
    u = ratio * ratio * ratio
    w = jnp.maximum(CUTOFF_SQ - q, 0.0)
    t = h * w + (1.0 / 3.0)
    near = (well * u) * ((u - 0.5) * t - (1.0 / 6.0))
    far = (charge * root) * (t + (11.0 / 3.0))
    g = (near + far) * w
    if allowed is not None:
        g = jnp.where(allowed, g, 0.0)
    high = g.astype(jnp.bfloat16)
    low = (g - high.astype(jnp.float32)).astype(jnp.bfloat16)
    return high, low


def both_sums(first, second, high, low):
    high_low = jnp.concatenate([high, low], axis=1)
    on_first = lax.dot_general(
        jnp.concatenate([second, second], axis=1), high_low, (((1,), (1,)), ((), ())),
        preferred_element_type=jnp.float32,
    )
    on_second = jnp.dot(
        jnp.concatenate([first, first], axis=1), jnp.concatenate([high, low], axis=0),
        preferred_element_type=jnp.float32,
    )
    return on_first, on_second


def invert(slot, inv_ref):
    lane_id = lax.broadcasted_iota(jnp.int32, (16, LANES), 1)
    row_id = lax.broadcasted_iota(jnp.int32, (16, LANES), 0)
    atom_id = lax.broadcasted_iota(jnp.int32, (LANES, LANES), 0)
    for a in range(BLOCKS):
        found = jnp.zeros((16, LANES), jnp.float32)
        for b in range(BLOCKS):
            hit = jnp.where(
                jnp.broadcast_to(slot[b : b + 1], (LANES, LANES)) == atom_id + a * LANES, 1.0, 0.0
            ).astype(jnp.bfloat16)
            names = jnp.where(row_id == 0, lane_id.astype(jnp.float32), float(b))
            found += lax.dot_general(
                names.astype(jnp.bfloat16), hit, (((1,), (1,)), ((), ())),
                preferred_element_type=jnp.float32,
            )
        whole = found[0:1] + LANES * found[1:2]
        inv_ref[a : a + 1, :] = whole.astype(jnp.int32)


def own_pairs(own, excl_ref, table, own_ref):
    place_i = lax.broadcasted_iota(jnp.int32, (LANES, LANES), 0)
    place_j = lax.broadcasted_iota(jnp.int32, (LANES, LANES), 1)
    gap = place_j - place_i
    excl = excl_ref[...]
    half_i = lax.broadcasted_iota(jnp.int32, (LANES, 64), 0) >> 1
    half_k = lax.broadcasted_iota(jnp.int32, (LANES, 64), 1)
    pick = half_i == half_k
    for b in range(BLOCKS):
        words = jnp.broadcast_to(excl[b : b + 1], (LANES, 64))
        word = jnp.sum(jnp.where(pick, words >> 15, 0).astype(jnp.float32), axis=1, keepdims=True)
        word_low = jnp.sum(
            jnp.where(pick, words & 32767, 0).astype(jnp.float32), axis=1, keepdims=True
        )
        odd = lax.broadcasted_iota(jnp.int32, (LANES, 1), 0) & 1
        mine15 = jnp.where(odd == 1, word, word_low).astype(jnp.int32)
        bits = (jnp.broadcast_to(mine15, (LANES, LANES)) >> jnp.clip(gap - 1, 0, 14)) & 1
        allowed = (gap >= 1) & ((gap > 15) | (bits == 0))
        value = block_rows([part[b : b + 1] for part in own], table)
        pieces = split(value)
        right = right_side(split(value * product_scale(1.0)))
        high, low = pair_strength(left_side(pieces), right, allowed)
        names = jnp.concatenate(pieces[:2], axis=0).astype(jnp.bfloat16)
        on_first, on_second = both_sums(names, names, high, low)
        own_ref[b * 16 : (b + 1) * 16, :] = on_first + on_second


def force_kernel(
    n_row, n_col, meta_ref, all_ref, sigma_ref, well_ref, charge_ref,
    own_ref, force_ref, sums_ref, first_list, second_list,
):
    mine = meta_ref[0, 3, 0]
    n_dev = n_row * n_col

    table = type_rows(sigma_ref, well_ref, charge_ref)

    def clear(n, _):
        sums_ref[pl.ds(n * 128, 128), :] = jnp.zeros((128, LANES), jnp.float32)
        return 0

    lax.fori_loop(0, n_dev, clear, 0)
    sums_ref[pl.ds(mine * 128, 128), :] = own_ref[...]

    total = lax.fori_loop(0, n_dev, lambda n, t: t + meta_ref[n, 2, 0], 0)
    start = mine * total // n_dev
    stop = (mine + 1) * total // n_dev

    def list_device(n, before):
        count = meta_ref[n, 2, 0]
        row, col = n // n_col, n % n_col

        def list_pair(s, _):
            p, q = meta_ref[n, 0, s], meta_ref[n, 1, s]
            at = before + s - start
            first_list[at] = row * (BLOCKS * n_col) + p
            second_list[at] = ((q >> 3) * n_col + col) * BLOCKS + (q & 7)
            return 0

        low = jnp.maximum(start - before, 0)
        high = jnp.minimum(count, stop - before)
        lax.fori_loop(low, high, list_pair, 0)
        return before + count

    lax.fori_loop(0, n_dev, list_device, 0)
    for extra in range(UNROLL):
        first_list[stop - start + extra] = 0
        second_list[stop - start + extra] = 0

    def add_tiles(step, _):
        found = []
        for extra in range(UNROLL):
            at = step * UNROLL + extra
            a, b = first_list[at], second_list[at]
            weight = (at < stop - start).astype(jnp.float32)
            first = split(load_block(all_ref, table, a >> 3, a & 7))
            second = split(load_block(all_ref, table, b >> 3, b & 7) * product_scale(weight))
            high, low = pair_strength(left_side(first), right_side(second))
            names = [
                jnp.concatenate(pieces[:2], axis=0).astype(jnp.bfloat16)
                for pieces in (first, second)
            ]
            found.append((a, b) + both_sums(names[0], names[1], high, low))
        for a, b, on_first, on_second in found:
            sums_ref[pl.ds(a * 16, 16), :] += on_first
            sums_ref[pl.ds(b * 16, 16), :] += on_second
        return 0

    lax.fori_loop(0, (stop - start + UNROLL - 1) // UNROLL, add_tiles, 0)

    def finish(n, _):
        def rows(r):
            return sums_ref[pl.ds(n * 128 + r, BLOCKS, stride=16), :]

        g_sum = rows(4)
        for comp in range(3):
            x = all_ref[pl.ds(n * ROWS + comp * BLOCKS, BLOCKS), :]
            force_ref[n, comp * BLOCKS : (comp + 1) * BLOCKS, :] = (
                x * g_sum - rows(comp) - rows(comp + 8)
            )
        return 0

    lax.fori_loop(0, n_dev, finish, 0)


def return_kernel(
    n_row, n_col, force_ref, inv_ref, out_ref,
    core_buf, send_buf, row_buf, core_send, core_recv, row_send, row_recv,
):
    row, col = lax.axis_index("row"), lax.axis_index("col")
    barrier = greet_peers(n_row, n_col)
    pl.semaphore_wait(barrier, n_row - 1 + n_col - 1)
    sends = []
    order = list(range(1, n_row)) + [0]
    for k in order:
        to_row = lax.rem(row + k, n_row)
        for j in range(1, n_col):
            to_col = lax.rem(col + j, n_col)
            there = pltpu.make_async_remote_copy(
                src_ref=force_ref.at[to_row * n_col + to_col],
                dst_ref=core_buf.at[k, j],
                send_sem=core_send.at[k, j],
                recv_sem=core_recv.at[k, j],
                device_id={"col": to_col},
                device_id_type=MESH,
            )
            there.start()
            sends.append(there)
    arrive = []
    own = None
    at = 0
    for k in order:
        to_row = lax.rem(row + k, n_row)
        part = force_ref[to_row * n_col + col]
        for j in range(1, n_col):
            sends[at].wait_recv()
            at += 1
            part = part + core_buf[k, j]
        if k == 0:
            own = part
        else:
            send_buf[k] = part
            there = pltpu.make_async_remote_copy(
                src_ref=send_buf.at[k],
                dst_ref=row_buf.at[k],
                send_sem=row_send.at[k],
                recv_sem=row_recv.at[k],
                device_id={"row": to_row},
                device_id_type=MESH,
            )
            there.start()
            arrive.append(there)
    for k in range(1, n_row):
        arrive[k - 1].wait_recv()
        own = own + row_buf[k]
    for there in sends + arrive:
        there.wait_send()
    inverse = inv_ref[...]
    lane, chunk = inverse & (LANES - 1), inverse >> 7
    for comp in range(3):
        total = jnp.zeros((BLOCKS, LANES), jnp.float32)
        for r in range(BLOCKS):
            at = comp * BLOCKS + r
            source = jnp.broadcast_to(own[at : at + 1], (BLOCKS, LANES))
            total = jnp.where(chunk == r, lane_gather(source, lane), total)
        for r in range(BLOCKS):
            out_ref[comp : comp + 1, r * LANES : (r + 1) * LANES] = total[r : r + 1]


def body(n_row, n_col, coords, atom_types, slot_atom, block_pairs, pair_count, exclusion,
         sigma_type, well_type, charge_type):
    n_dev = n_row * n_col
    slots = slot_atom.reshape(BLOCKS, LANES)
    vmem = pl.BlockSpec(memory_space=pltpu.VMEM)
    smem = pl.BlockSpec(memory_space=pltpu.SMEM)
    dma = pltpu.SemaphoreType.DMA
    tables = [t.reshape(1, LANES) for t in (sigma_type, well_type, charge_type)]
    arrays = [
        coords, atom_types.reshape(BLOCKS, LANES), slots, block_pairs, exclusion, *tables
    ]
    gathered, meta, own, inverse = pl.pallas_call(
        functools.partial(exchange_kernel, n_row, n_col),
        out_shape=(
            jax.ShapeDtypeStruct((n_dev, ROWS, LANES), jnp.float32),
            jax.ShapeDtypeStruct((n_dev, 8, LANES), jnp.int32),
            jax.ShapeDtypeStruct((BLOCKS * 16, LANES), jnp.float32),
            jax.ShapeDtypeStruct((BLOCKS, LANES), jnp.int32),
        ),
        in_specs=[smem] + [pl.BlockSpec(memory_space=pltpu.HBM)] * 8,
        out_specs=(vmem,) * 4,
        scratch_shapes=[pltpu.VMEM(a.shape, a.dtype) for a in arrays] + [
            dma((8,)), dma((n_row,)), dma((n_row,)), dma((n_row, n_col)), dma((n_row, n_col)),
        ],
        compiler_params=pltpu.CompilerParams(
            collective_id=0, has_side_effects=True, vmem_limit_bytes=63 << 20
        ),
        name="exchange",
    )(pair_count, *arrays)
    most = block_pairs.shape[1]
    force = pl.pallas_call(
        functools.partial(force_kernel, n_row, n_col),
        out_shape=jax.ShapeDtypeStruct((n_dev, 24, LANES), jnp.float32),
        in_specs=[smem] + [vmem] * 5,
        out_specs=vmem,
        scratch_shapes=[
            pltpu.VMEM((n_dev * 128, LANES), jnp.float32),
            pltpu.SMEM((most + 1 + UNROLL,), jnp.int32),
            pltpu.SMEM((most + 1 + UNROLL,), jnp.int32),
        ],
        compiler_params=pltpu.CompilerParams(vmem_limit_bytes=63 << 20),
        name="pair_forces",
    )(
        meta, gathered.reshape(n_dev * ROWS, LANES), *tables, own,
    )
    return pl.pallas_call(
        functools.partial(return_kernel, n_row, n_col),
        out_shape=jax.ShapeDtypeStruct(coords.shape, jnp.float32),
        in_specs=[vmem, vmem],
        out_specs=vmem,
        scratch_shapes=[
            pltpu.VMEM((n_row, n_col, 24, LANES), jnp.float32),
            pltpu.VMEM((n_row, 24, LANES), jnp.float32),
            pltpu.VMEM((n_row, 24, LANES), jnp.float32),
            dma((n_row, n_col)), dma((n_row, n_col)), dma((n_row,)), dma((n_row,)),
        ],
        compiler_params=pltpu.CompilerParams(
            collective_id=1, has_side_effects=True, vmem_limit_bytes=32 << 20
        ),
        name="return_forces",
    )(force, inverse)


def solution(mesh):
    every = ("groups", "row", "col")
    return jax.shard_map(
        functools.partial(body, mesh.shape["row"], mesh.shape["col"]),
        mesh=mesh,
        in_specs=(
            P(None, every), P(every), P(every), P(None, every), P(every), P(every, None),
            P(), P(), P(),
        ),
        out_specs=P(None, every),
        check_vma=False,
    )
```

```python
import functools

import jax
import jax.numpy as jnp
from jax import lax
from jax.experimental import pallas as pl
from jax.experimental.pallas import tpu as pltpu
from jax.sharding import PartitionSpec as P

COULOMB = 83.0159
CUTOFF_SQ = 144.0
CENTER = 12.0
LANES = 128
BLOCKS = 8
ROWS = 40
UNROLL = 8
MESH = pl.DeviceIdType.MESH


def lane_gather(table, lanes):
    return jnp.take_along_axis(table, lanes, axis=1, mode="promise_in_bounds")


def greet_peers(n_row, n_col):
    row, col = lax.axis_index("row"), lax.axis_index("col")
    barrier = pltpu.get_barrier_semaphore()
    for k in range(1, n_row):
        pl.semaphore_signal(
            barrier, inc=1, device_id={"row": lax.rem(row + k, n_row)}, device_id_type=MESH
        )
    for k in range(1, n_col):
        pl.semaphore_signal(
            barrier, inc=1, device_id={"col": lax.rem(col + k, n_col)}, device_id_type=MESH
        )
    return barrier


def exchange_kernel(
    n_row, n_col, count_ref, *refs,
):
    inputs, (all_ref, meta_ref, own_ref, inv_ref), local = refs[:8], refs[8:12], refs[12:20]
    load_sem, send_sem, recv_sem, pass_send, pass_recv = refs[20:]
    loads = [
        pltpu.make_async_copy(source, target, load_sem.at[k])
        for k, (source, target) in enumerate(zip(inputs, local))
    ]
    for load in loads:
        load.start()
    coords_ref, types_ref, slot_ref, pairs_ref, excl_ref, sigma_ref, well_ref, charge_ref = local
    row, col = lax.axis_index("row"), lax.axis_index("col")
    barrier = greet_peers(n_row, n_col)
    for load in loads:
        load.wait()
    slot = slot_ref[...]
    own = []
    lane, chunk = slot & (LANES - 1), slot >> 7
    mine = row * n_col + col
    kinds = types_ref[...].astype(jnp.float32)
    for comp in range(4):
        total = jnp.zeros((BLOCKS, LANES), jnp.float32)
        for r in range(BLOCKS):
            if comp < 3:
                source = coords_ref[comp : comp + 1, r * LANES : (r + 1) * LANES] - CENTER
            else:
                source = kinds[r : r + 1]
            source = jnp.broadcast_to(source, (BLOCKS, LANES))
            total = jnp.where(chunk == r, lane_gather(source, lane), total)
        all_ref[mine, comp * BLOCKS : (comp + 1) * BLOCKS, :] = total
        own.append(total)
    pairs = pairs_ref[...].astype(jnp.float32)
    count = jnp.full((1, LANES), count_ref[0], jnp.int32).astype(jnp.float32)
    all_ref[mine, 32:40, :] = jnp.concatenate(
        [pairs, count, jnp.zeros((5, LANES), jnp.float32)], axis=0
    )

    pl.semaphore_wait(barrier, n_row - 1 + n_col - 1)

    def copy(slot_index, target, sems):
        return pltpu.make_async_remote_copy(
            src_ref=all_ref.at[slot_index],
            dst_ref=all_ref.at[slot_index],
            send_sem=sems[0],
            recv_sem=sems[1],
            device_id=target,
            device_id_type=MESH,
        )

    sends, passes = [], []
    for k in range(1, n_row):
        there = copy(mine, {"row": lax.rem(row + k, n_row)}, (send_sem.at[k], recv_sem.at[k]))
        there.start()
        sends.append(there)
    for k in range(n_row):
        from_row = lax.rem(row + n_row - k, n_row)
        if k == 1:
            own_pairs(own, excl_ref, type_rows(sigma_ref, well_ref, charge_ref), own_ref)
        if k:
            copy(
                from_row * n_col + col, {"row": from_row}, (send_sem.at[k], recv_sem.at[k])
            ).wait_recv()
        for j in range(1, n_col):
            on = copy(
                from_row * n_col + col,
                {"col": lax.rem(col + j, n_col)},
                (pass_send.at[k, j], pass_recv.at[k, j]),
            )
            on.start()
            passes.append(on)
    invert(slot, inv_ref)
    for k in range(n_row):
        from_row = lax.rem(row + n_row - k, n_row)
        for j in range(1, n_col):
            from_col = lax.rem(col + n_col - j, n_col)
            copy(
                from_row * n_col + from_col,
                {"col": from_col},
                (pass_send.at[k, j], pass_recv.at[k, j]),
            ).wait_recv()
    for there in sends + passes:
        there.wait_send()
    meta_ref[...] = all_ref[:, 32:40, :].astype(jnp.int32)
    meta_ref[0, 3:4, :] = jnp.full((1, LANES), mine, jnp.int32)


def split(value):
    high = value.astype(jnp.bfloat16).astype(jnp.float32)
    rest = value - high
    mid = rest.astype(jnp.bfloat16).astype(jnp.float32)
    return high, mid, rest - mid


def row_mask(*rows):
    index = lax.broadcasted_iota(jnp.int32, (8, LANES), 0)
    hit = index == rows[0]
    for r in rows[1:]:
        hit = hit | (index == r)
    return hit


def product_scale(weight):
    index = lax.broadcasted_iota(jnp.int32, (8, LANES), 0)
    well_scale = (4.0 * 12.0 / (CUTOFF_SQ * CUTOFF_SQ)) * weight
    charge_scale = (COULOMB / (CUTOFF_SQ * CUTOFF_SQ)) * weight
    return jnp.where(index == 6, well_scale, jnp.where(index == 7, charge_scale, 1.0))


def type_rows(sigma_ref, well_ref, charge_ref):
    return jnp.concatenate(
        [
            jnp.zeros((5, LANES), jnp.float32),
            0.5 * sigma_ref[...],
            well_ref[...],
            charge_ref[...],
        ],
        axis=0,
    )


def load_block(all_ref, table, device, block):
    return block_rows(
        [all_ref[pl.ds(device * ROWS + block + 8 * comp, 1), :] for comp in range(4)], table
    )


def block_rows(parts, table):
    x, y, z, kind = parts
    kind = kind.astype(jnp.int32)
    params = lane_gather(table, jnp.broadcast_to(kind, (8, LANES)))
    index = lax.broadcasted_iota(jnp.int32, (8, LANES), 0)
    norm = x * x + y * y + z * z
    value = jnp.where(index == 0, x, params)
    value = jnp.where(index == 1, y, value)
    value = jnp.where(index == 2, z, value)
    value = jnp.where(index == 3, norm, value)
    return jnp.where(index == 4, 1.0, value)


def left_side(pieces):
    high, mid, low = pieces
    return jnp.concatenate([high, high, mid, mid, high, low], axis=0)


def right_side(pieces):
    index = lax.broadcasted_iota(jnp.int32, (8, LANES), 0)
    high, mid, low = pieces
    parts = []
    for piece in (high, mid, low):
        one = 1.0 if piece is high else 0.0
        for_q = jnp.where(index < 3, -2.0 * piece, 0.0)
        for_q = jnp.where(index == 3, one, for_q)
        for_q = jnp.where(index == 4, jnp.broadcast_to(piece[3:4], (8, LANES)), for_q)
        for_s = jnp.where(index == 5, one, 0.0)
        for_s = jnp.where(index == 4, jnp.broadcast_to(piece[5:6], (8, LANES)), for_s)
        for_well = jnp.where(index == 6, piece, 0.0)
        for_charge = jnp.where(index == 7, piece, 0.0)
        parts.append(jnp.concatenate([for_q, for_s, for_well, for_charge], axis=1))
    high, mid, low = parts
    return jnp.concatenate([high, mid, high, mid, low, high], axis=0)


def pair_strength(left, right, allowed=None):
    both = jnp.dot(
        left.T.astype(jnp.bfloat16), right.astype(jnp.bfloat16),
        preferred_element_type=jnp.float32,
    )
    q, s = both[:, :LANES], both[:, LANES : 2 * LANES]
    well, charge = both[:, 2 * LANES : 3 * LANES], both[:, 3 * LANES :]
    s_sq = s * s
    root = lax.rsqrt(q + s_sq)
    h = root * root
    ratio = s_sq * h
    u = ratio * ratio * ratio
    w = jnp.maximum(CUTOFF_SQ - q, 0.0)
    t = h * w + (1.0 / 3.0)
    near = (well * u) * ((u - 0.5) * t - (1.0 / 6.0))
    far = (charge * root) * (t + (11.0 / 3.0))
    g = (near + far) * w
    if allowed is not None:
        g = jnp.where(allowed, g, 0.0)
    high = g.astype(jnp.bfloat16)
    low = (g - high.astype(jnp.float32)).astype(jnp.bfloat16)
    return high, low


def both_sums(first, second, high, low):
    high_low = jnp.concatenate([high, low], axis=1)
    on_first = lax.dot_general(
        jnp.concatenate([second, second], axis=1), high_low, (((1,), (1,)), ((), ())),
        preferred_element_type=jnp.float32,
    )
    on_second = jnp.dot(
        jnp.concatenate([first, first], axis=1), jnp.concatenate([high, low], axis=0),
        preferred_element_type=jnp.float32,
    )
    return on_first, on_second


def invert(slot, inv_ref):
    lane_id = lax.broadcasted_iota(jnp.int32, (16, LANES), 1)
    row_id = lax.broadcasted_iota(jnp.int32, (16, LANES), 0)
    atom_id = lax.broadcasted_iota(jnp.int32, (LANES, LANES), 0)
    for a in range(BLOCKS):
        found = jnp.zeros((16, LANES), jnp.float32)
        for b in range(BLOCKS):
            hit = jnp.where(
                jnp.broadcast_to(slot[b : b + 1], (LANES, LANES)) == atom_id + a * LANES, 1.0, 0.0
            ).astype(jnp.bfloat16)
            names = jnp.where(row_id == 0, lane_id.astype(jnp.float32), float(b))
            found += lax.dot_general(
                names.astype(jnp.bfloat16), hit, (((1,), (1,)), ((), ())),
                preferred_element_type=jnp.float32,
            )
        whole = found[0:1] + LANES * found[1:2]
        inv_ref[a : a + 1, :] = whole.astype(jnp.int32)


def own_pairs(own, excl_ref, table, own_ref):
    place_i = lax.broadcasted_iota(jnp.int32, (LANES, LANES), 0)
    place_j = lax.broadcasted_iota(jnp.int32, (LANES, LANES), 1)
    gap = place_j - place_i
    excl = excl_ref[...]
    half_i = lax.broadcasted_iota(jnp.int32, (LANES, 64), 0) >> 1
    half_k = lax.broadcasted_iota(jnp.int32, (LANES, 64), 1)
    pick = half_i == half_k
    for b in range(BLOCKS):
        words = jnp.broadcast_to(excl[b : b + 1], (LANES, 64))
        word = jnp.sum(jnp.where(pick, words >> 15, 0).astype(jnp.float32), axis=1, keepdims=True)
        word_low = jnp.sum(
            jnp.where(pick, words & 32767, 0).astype(jnp.float32), axis=1, keepdims=True
        )
        odd = lax.broadcasted_iota(jnp.int32, (LANES, 1), 0) & 1
        mine15 = jnp.where(odd == 1, word, word_low).astype(jnp.int32)
        bits = (jnp.broadcast_to(mine15, (LANES, LANES)) >> jnp.clip(gap - 1, 0, 14)) & 1
        allowed = (gap >= 1) & ((gap > 15) | (bits == 0))
        value = block_rows([part[b : b + 1] for part in own], table)
        pieces = split(value)
        right = right_side(split(value * product_scale(1.0)))
        high, low = pair_strength(left_side(pieces), right, allowed)
        names = jnp.concatenate(pieces[:2], axis=0).astype(jnp.bfloat16)
        on_first, on_second = both_sums(names, names, high, low)
        own_ref[b * 16 : (b + 1) * 16, :] = on_first + on_second


def force_kernel(
    n_row, n_col, meta_ref, all_ref, sigma_ref, well_ref, charge_ref,
    own_ref, force_ref, sums_ref, first_list, second_list,
):
    mine = meta_ref[0, 3, 0]
    n_dev = n_row * n_col

    table = type_rows(sigma_ref, well_ref, charge_ref)

    def clear(n, _):
        sums_ref[pl.ds(n * 128, 128), :] = jnp.zeros((128, LANES), jnp.float32)
        return 0

    lax.fori_loop(0, n_dev, clear, 0)
    sums_ref[pl.ds(mine * 128, 128), :] = own_ref[...]

    total = lax.fori_loop(0, n_dev, lambda n, t: t + meta_ref[n, 2, 0], 0)
    start = mine * total // n_dev
    stop = (mine + 1) * total // n_dev

    def list_device(n, before):
        count = meta_ref[n, 2, 0]
        row, col = n // n_col, n % n_col

        def list_pair(s, _):
            p, q = meta_ref[n, 0, s], meta_ref[n, 1, s]
            at = before + s - start
            first_list[at] = row * (BLOCKS * n_col) + p
            second_list[at] = ((q >> 3) * n_col + col) * BLOCKS + (q & 7)
            return 0

        low = jnp.maximum(start - before, 0)
        high = jnp.minimum(count, stop - before)
        lax.fori_loop(low, high, list_pair, 0)
        return before + count

    lax.fori_loop(0, n_dev, list_device, 0)
    for extra in range(UNROLL):
        first_list[stop - start + extra] = 0
        second_list[stop - start + extra] = 0

    def add_tiles(step, _):
        found = []
        for extra in range(UNROLL):
            at = step * UNROLL + extra
            a, b = first_list[at], second_list[at]
            weight = (at < stop - start).astype(jnp.float32)
            first = split(load_block(all_ref, table, a >> 3, a & 7))
            second = split(load_block(all_ref, table, b >> 3, b & 7) * product_scale(weight))
            high, low = pair_strength(left_side(first), right_side(second))
            names = [
                jnp.concatenate(pieces[:2], axis=0).astype(jnp.bfloat16)
                for pieces in (first, second)
            ]
            found.append((a, b) + both_sums(names[0], names[1], high, low))
        for a, b, on_first, on_second in found:
            sums_ref[pl.ds(a * 16, 16), :] += on_first
            sums_ref[pl.ds(b * 16, 16), :] += on_second
        return 0

    lax.fori_loop(0, (stop - start + UNROLL - 1) // UNROLL, add_tiles, 0)

    def finish(n, _):
        def rows(r):
            return sums_ref[pl.ds(n * 128 + r, BLOCKS, stride=16), :]

        g_sum = rows(4)
        for comp in range(3):
            x = all_ref[pl.ds(n * ROWS + comp * BLOCKS, BLOCKS), :]
            force_ref[n, comp * BLOCKS : (comp + 1) * BLOCKS, :] = (
                x * g_sum - rows(comp) - rows(comp + 8)
            )
        return 0

    lax.fori_loop(0, n_dev, finish, 0)


def return_kernel(
    n_row, n_col, force_ref, inv_ref, out_ref,
    core_buf, send_buf, row_buf, part_buf, part_sem, core_send, core_recv, row_send, row_recv,
):
    row, col = lax.axis_index("row"), lax.axis_index("col")
    barrier = greet_peers(n_row, n_col)
    parts = [
        pltpu.make_async_copy(
            force_ref.at[lax.rem(row + k, n_row) * n_col + col], part_buf.at[k], part_sem.at[k]
        )
        for k in range(n_row)
    ]
    for part in parts:
        part.start()
    pl.semaphore_wait(barrier, n_row - 1 + n_col - 1)
    sends = []
    order = list(range(1, n_row)) + [0]
    for k in order:
        to_row = lax.rem(row + k, n_row)
        for j in range(1, n_col):
            to_col = lax.rem(col + j, n_col)
            there = pltpu.make_async_remote_copy(
                src_ref=force_ref.at[to_row * n_col + to_col],
                dst_ref=core_buf.at[k, j],
                send_sem=core_send.at[k, j],
                recv_sem=core_recv.at[k, j],
                device_id={"col": to_col},
                device_id_type=MESH,
            )
            there.start()
            sends.append(there)
    arrive = []
    own = None
    at = 0
    for k in order:
        to_row = lax.rem(row + k, n_row)
        parts[k].wait()
        part = part_buf[k]
        for j in range(1, n_col):
            sends[at].wait_recv()
            at += 1
            part = part + core_buf[k, j]
        if k == 0:
            own = part
        else:
            send_buf[k] = part
            there = pltpu.make_async_remote_copy(
                src_ref=send_buf.at[k],
                dst_ref=row_buf.at[k],
                send_sem=row_send.at[k],
                recv_sem=row_recv.at[k],
                device_id={"row": to_row},
                device_id_type=MESH,
            )
            there.start()
            arrive.append(there)
    for k in range(1, n_row):
        arrive[k - 1].wait_recv()
        own = own + row_buf[k]
    for there in sends + arrive:
        there.wait_send()
    inverse = inv_ref[...]
    lane, chunk = inverse & (LANES - 1), inverse >> 7
    for comp in range(3):
        total = jnp.zeros((BLOCKS, LANES), jnp.float32)
        for r in range(BLOCKS):
            at = comp * BLOCKS + r
            source = jnp.broadcast_to(own[at : at + 1], (BLOCKS, LANES))
            total = jnp.where(chunk == r, lane_gather(source, lane), total)
        for r in range(BLOCKS):
            out_ref[comp : comp + 1, r * LANES : (r + 1) * LANES] = total[r : r + 1]


def body(n_row, n_col, coords, atom_types, slot_atom, block_pairs, pair_count, exclusion,
         sigma_type, well_type, charge_type):
    n_dev = n_row * n_col
    slots = slot_atom.reshape(BLOCKS, LANES)
    vmem = pl.BlockSpec(memory_space=pltpu.VMEM)
    smem = pl.BlockSpec(memory_space=pltpu.SMEM)
    dma = pltpu.SemaphoreType.DMA
    tables = [t.reshape(1, LANES) for t in (sigma_type, well_type, charge_type)]
    arrays = [
        coords, atom_types.reshape(BLOCKS, LANES), slots, block_pairs, exclusion, *tables
    ]
    gathered, meta, own, inverse = pl.pallas_call(
        functools.partial(exchange_kernel, n_row, n_col),
        out_shape=(
            jax.ShapeDtypeStruct((n_dev, ROWS, LANES), jnp.float32),
            jax.ShapeDtypeStruct((n_dev, 8, LANES), jnp.int32),
            jax.ShapeDtypeStruct((BLOCKS * 16, LANES), jnp.float32),
            jax.ShapeDtypeStruct((BLOCKS, LANES), jnp.int32),
        ),
        in_specs=[smem] + [pl.BlockSpec(memory_space=pltpu.HBM)] * 8,
        out_specs=(vmem,) * 4,
        scratch_shapes=[pltpu.VMEM(a.shape, a.dtype) for a in arrays] + [
            dma((8,)), dma((n_row,)), dma((n_row,)), dma((n_row, n_col)), dma((n_row, n_col)),
        ],
        compiler_params=pltpu.CompilerParams(
            collective_id=0, has_side_effects=True, vmem_limit_bytes=63 << 20
        ),
        name="exchange",
    )(pair_count, *arrays)
    most = block_pairs.shape[1]
    force = pl.pallas_call(
        functools.partial(force_kernel, n_row, n_col),
        out_shape=jax.ShapeDtypeStruct((n_dev, 24, LANES), jnp.float32),
        in_specs=[smem] + [vmem] * 5,
        out_specs=vmem,
        scratch_shapes=[
            pltpu.VMEM((n_dev * 128, LANES), jnp.float32),
            pltpu.SMEM((most + 1 + UNROLL,), jnp.int32),
            pltpu.SMEM((most + 1 + UNROLL,), jnp.int32),
        ],
        compiler_params=pltpu.CompilerParams(vmem_limit_bytes=63 << 20),
        name="pair_forces",
    )(
        meta, gathered.reshape(n_dev * ROWS, LANES), *tables, own,
    )
    return pl.pallas_call(
        functools.partial(return_kernel, n_row, n_col),
        out_shape=jax.ShapeDtypeStruct(coords.shape, jnp.float32),
        in_specs=[pl.BlockSpec(memory_space=pltpu.HBM), vmem],
        out_specs=vmem,
        scratch_shapes=[
            pltpu.VMEM((n_row, n_col, 24, LANES), jnp.float32),
            pltpu.VMEM((n_row, 24, LANES), jnp.float32),
            pltpu.VMEM((n_row, 24, LANES), jnp.float32),
            pltpu.VMEM((n_row, 24, LANES), jnp.float32),
            dma((n_row,)), dma((n_row, n_col)), dma((n_row, n_col)), dma((n_row,)), dma((n_row,)),
        ],
        compiler_params=pltpu.CompilerParams(
            collective_id=1, has_side_effects=True, vmem_limit_bytes=63 << 20
        ),
        name="return_forces",
    )(force, inverse)


def solution(mesh):
    every = ("groups", "row", "col")
    return jax.shard_map(
        functools.partial(body, mesh.shape["row"], mesh.shape["col"]),
        mesh=mesh,
        in_specs=(
            P(None, every), P(every), P(every), P(None, every), P(every), P(every, None),
            P(), P(), P(),
        ),
        out_specs=P(None, every),
        check_vma=False,
    )
```
